32 devices in a mesh: seq: 8 (over z, y), txt: 4 (over x, core).
Axes of the slice: x: 2, y: 2, z: 4, core: 2. Of those that a mesh axis runs over, the one named last changes fastest.
Arguments:
- self_q: bfloat16 [3072, 1024], P('seq', 'txt'), may hold values from -8 to 8
- self_k: bfloat16 [3072, 1024], P('seq', 'txt'), may hold values from -8 to 8
- self_v: bfloat16 [3072, 1024], P('seq', 'txt'), may hold values from -6 to 6
- cross_q: bfloat16 [3072, 1024], P('seq', 'txt'), may hold values from -8 to 8
- text_k: bfloat16 [4096, 1024], P('txt'), may hold values from -8 to 8
- text_v: bfloat16 [4096, 1024], P('txt'), may hold values from -6 to 6
- lags: int32 [24], P('seq'), may hold values from 1 to 32, as said below
Outputs:
- self_out: bfloat16 [3072, 1024], P('seq', 'txt')
- cross_out: bfloat16 [3072, 1024], P('seq', 'txt')
The draws below stay inside these ranges and needn't reach their ends.
Inputs may be any that keep to these rules, and one draw needn't show every extreme that they name: lags never fall from one span to the next; the last span sees all 32 blocks.
All inputs are finite; a program needn't handle non-finite values.
Results may differ from the reference program's by a relative error of at most 0.014.
Values may be sent and summed in bfloat16 or wider, within the bound.
A program may use at most 128 MiB of HBM per device.

```python
import math
import jax
import jax.numpy as jnp
from jax import lax

HEADS = 8
HSIZE = 128
SPAN = 128
TBLK = 128
FRAMES = 3072
TEXT = 4096
HD = 1024


def drawn_draw(key, rows, salt):
    width = HEADS * HSIZE
    base = jax.random.normal(jax.random.fold_in(key, salt), (rows, width), jnp.float32)
    return jnp.clip(base, -8.0, 8.0).astype(jnp.bfloat16)


def draw_self_q(key, part):
    return drawn_draw(key, FRAMES, 11)


def draw_self_k(key, part):
    return drawn_draw(key, FRAMES, 23)


def draw_cross_q(key, part):
    return drawn_draw(key, FRAMES, 37)


def draw_text_k(key, part):
    return drawn_draw(key, TEXT, 53)


def draw_lags(key, part):
    count = FRAMES // SPAN
    top = TEXT // TBLK
    steps = jax.random.randint(jax.random.fold_in(key, 71), (count,), 1, 5)
    running = jnp.cumsum(steps)
    return (1 + (top - 1) * running // running[-1]).astype(jnp.int32)


def levels(stream_key, shape, pieces, smallest, largest):
    gain, own = 1.0, jax.random.fold_in(stream_key, 6)
    for axis_at, parts in pieces:
        heights = jnp.exp(jax.random.uniform(jax.random.fold_in(own, axis_at), (parts,), jnp.float32, smallest / len(pieces), largest / len(pieces)))
        gain = gain * jnp.repeat(heights, shape[axis_at] // parts).reshape([-1 if axis == axis_at else 1 for axis in range(len(shape))])
    return gain


def gaussian(own_key, shape, spread, most, shards=(), kind=jnp.bfloat16):
    array = jax.random.normal(own_key, shape, jnp.float32) * spread
    if len(shards) > 0:
        array = levels(own_key, shape, shards, -0.22, 0.18) * array
    return jnp.clip(array, min=-most, max=most).astype(kind)


def setup_inputs(seed: int = 0) -> dict:
    seeds = jax.random.split(jax.random.key(seed), 8)
    return {
        "self_q": draw_self_q(jax.random.fold_in(seeds[7], 71), 0),
        "self_k": draw_self_k(jax.random.fold_in(seeds[7], 71), 0),
        "self_v": gaussian(seeds[2], (FRAMES, HD), 1.0, 6.0, ((0, 8), (1, 4))),
        "cross_q": draw_cross_q(jax.random.fold_in(seeds[7], 71), 0),
        "text_k": draw_text_k(jax.random.fold_in(seeds[7], 71), 0),
        "text_v": gaussian(seeds[5], (TEXT, HD), 1.0, 6.0, ((0, 4),)),
        "lags": draw_lags(jax.random.fold_in(seeds[7], 71), 0),
    }


def attend(query, keys, values, visible):
    factor = 1.0 / math.sqrt(HSIZE)
    scores = jnp.einsum('qhd,khd->hqk', query.astype(jnp.float32), keys, preferred_element_type=jnp.float32) * factor
    scores = jnp.where(visible[None], scores, -jnp.inf)
    peak = lax.optimization_barrier(jnp.max(scores, axis=2))
    probs = jnp.exp(scores - peak[:, :, None])
    totals = lax.optimization_barrier(jnp.sum(probs, axis=2))
    weights = lax.optimization_barrier(probs.astype(jnp.bfloat16)).astype(jnp.float32)
    mixed = jnp.einsum('hqk,khd->qhd', weights, values, preferred_element_type=jnp.float32)
    mixed = mixed / jnp.transpose(totals)[:, :, None]
    return mixed.reshape(mixed.shape[0], HEADS * HSIZE).astype(jnp.bfloat16)

def reference(self_q, self_k, self_v, cross_q, text_k, text_v, lags):
    block = 512 if FRAMES % 512 == 0 else FRAMES
    count = FRAMES // block
    keys = self_k.astype(jnp.float32).reshape(FRAMES, HEADS, HSIZE)
    values = self_v.astype(jnp.float32).reshape(FRAMES, HEADS, HSIZE)
    text_keys = text_k.astype(jnp.float32).reshape(TEXT, HEADS, HSIZE)
    text_values = text_v.astype(jnp.float32).reshape(TEXT, HEADS, HSIZE)
    limits = (jnp.repeat(lags, SPAN) * TBLK).astype(jnp.int32)
    frame_pos = jnp.arange(FRAMES, dtype=jnp.int32)
    text_pos = jnp.arange(TEXT, dtype=jnp.int32)

    def self_block(number):
        first = (number * block).astype(jnp.int32)
        rows = lax.dynamic_slice_in_dim(self_q, first, block, 0).reshape(block, HEADS, HSIZE)
        query_pos = first + jnp.arange(block, dtype=jnp.int32)
        visible = frame_pos[None, :] <= query_pos[:, None]
        return attend(rows, keys, values, visible)

    def cross_block(number):
        first = (number * block).astype(jnp.int32)
        rows = lax.dynamic_slice_in_dim(cross_q, first, block, 0).reshape(block, HEADS, HSIZE)
        bound = lax.dynamic_slice_in_dim(limits, first, block, 0)
        visible = text_pos[None, :] < bound[:, None]
        return attend(rows, text_keys, text_values, visible)
    numbers = jnp.arange(count, dtype=jnp.int32)
    self_out = lax.map(self_block, numbers).reshape(FRAMES, HEADS * HSIZE)
    cross_out = lax.map(cross_block, numbers).reshape(FRAMES, HEADS * HSIZE)
    return (self_out, cross_out)
```

```python
import functools
import math

import jax
import jax.numpy as jnp
from jax import lax
from jax.experimental import pallas as pl
from jax.experimental.pallas import tpu as pltpu
from jax.sharding import PartitionSpec as P

HSIZE = 128
SPAN = 128
TBLK = 128

NEG = -1e30
FLOOR = -1e20
SCALE = math.log2(math.e) / math.sqrt(HSIZE)
MESH = pl.DeviceIdType.MESH


def scores_of(query, keys):
    return (
        lax.dot_general(
            query, keys, (((1,), (1,)), ((), ())), preferred_element_type=jnp.float32
        )
        * SCALE
    )


def pack_stats(columns):
    rows = columns[0].shape[0]
    lane = lax.broadcasted_iota(jnp.int32, (rows, HSIZE), 1)
    tile = jnp.zeros((rows, HSIZE), jnp.float32)
    for at, column in enumerate(columns):
        tile = jnp.where(lane == at, column, tile)
    return jnp.transpose(tile)[:8]


def unpack_stats(packed, count):
    full = jnp.concatenate(
        [packed, jnp.zeros((HSIZE - 8, packed.shape[1]), jnp.float32)], axis=0
    )
    tile = jnp.transpose(full)
    return [tile[:, at : at + 1] for at in range(count)]


def kernel(
    S, T, rows, H, text,
    lags, q, k, v, cq, tk, tv,
    self_out, cross_out,
    qp, kbuf, vbuf, acc, top, tot,
    pair_out, pair_in, pstat_out, pstat_in,
    cqb, tkb, tvb, cown, ctop, ctot,
    part_out, part_in, cstat_out, cstat_in,
    loc_sem, txt_sem, q_send, q_recv, kv_send, kv_recv,
    cq_send, cq_recv, pair_send, pair_recv, part_send, part_recv,
):
    me = lax.axis_index("seq")
    t = lax.axis_index("txt")
    nz = S // 2
    z = me // 2
    y = me % 2
    partner = me + 1 - 2 * y
    up = (me + 2) % S
    width = H * HSIZE

    if T == 4:
        peers = [t, t + 1 - 2 * (t % 2), t + 2 - 4 * (t // 2), 3 - t]
        owners = peers
    else:
        peers = [(t + r) % T for r in range(T)]
        owners = [(t + T - r) % T for r in range(T)]

    def cols(h):
        return pl.ds(h * HSIZE, HSIZE)

    locals_ = []

    def local(src, dst, sem):
        copy = pltpu.make_async_copy(src, dst, sem)
        copy.start()
        return copy

    own_cq = local(cq, cqb.at[0], loc_sem.at[0])
    text_copies = []
    for r in range(T):
        at = pl.ds(pl.multiple_of(owners[r] * width, HSIZE), width)
        text_copies.append(
            (
                local(tk.at[:, at], tkb.at[r], txt_sem.at[r, 0]),
                local(tv.at[:, at], tvb.at[r], txt_sem.at[r, 1]),
            )
        )
    for h in range(H):
        locals_.append(local(q.at[:, cols(h)], qp.at[h, pl.ds(0, rows)], loc_sem.at[1 + 3 * h]))
        locals_.append(local(k.at[:, cols(h)], kbuf.at[0, h], loc_sem.at[2 + 3 * h]))
        locals_.append(local(v.at[:, cols(h)], vbuf.at[0, h], loc_sem.at[3 + 3 * h]))

    barrier = pltpu.get_barrier_semaphore()
    pl.semaphore_signal(barrier, inc=1, device_id=(partner, t), device_id_type=MESH)
    for r in range(1, T):
        pl.semaphore_signal(barrier, inc=1, device_id=(me, peers[r]), device_id_type=MESH)

    @pl.when(z < nz - 1)
    def _():
        pl.semaphore_signal(barrier, inc=1, device_id=(me + 2, t), device_id_type=MESH)

    @pl.when(z > 0)
    def _():
        pl.semaphore_signal(barrier, inc=1, device_id=(me - 2, t), device_id_type=MESH)

    pl.semaphore_wait(barrier, T + jnp.minimum(z, 1) + jnp.minimum(nz - 1 - z, 1))

    def remote(src, dst, send, recv, device):
        return pltpu.make_async_remote_copy(
            src_ref=src, dst_ref=dst, send_sem=send, recv_sem=recv,
            device_id=device, device_id_type=MESH,
        )

    def kv_copy(d, h, which, src=None):
        buf = (kbuf, vbuf)[which]
        return remote(
            buf.at[d, h] if src is None else src, buf.at[d + 1, h],
            kv_send.at[d, h, which], kv_recv.at[d + 1, h, which], (up, t),
        )

    def own_kv(h, which):
        return kv_copy(0, h, which, (k, v)[which].at[:, cols(h)])

    @pl.when(z < nz - 1)
    def _():
        for h in range(H):
            own_kv(h, 0).start()
            own_kv(h, 1).start()

    q_copies = [
        remote(q.at[:, cols(h)], qp.at[h, pl.ds(rows, rows)], q_send.at[h], q_recv.at[h], (partner, t))
        for h in range(H)
    ]
    cq_copies = [None] + [
        remote(cq, cqb.at[r], cq_send.at[r], cq_recv.at[r], (me, peers[r])) for r in range(1, T)
    ]
    for r in range(1, T):
        cq_copies[r].start()
    for copy in q_copies:
        copy.start()

    row_id = lax.broadcasted_iota(jnp.int32, (rows, 1), 0)
    limit = jnp.full((rows, 1), lags[0] * TBLK, jnp.int32)
    for c in range(1, rows // SPAN):
        limit = jnp.where(row_id >= c * SPAN, lags[c] * TBLK, limit)
    limit = limit - t * text

    def cross_head(r, h):
        low = h * HSIZE
        s = scores_of(cqb[r, :, low : low + HSIZE], tkb[r, :, low : low + HSIZE])
        col = lax.broadcasted_iota(jnp.int32, (rows, text), 1)
        s = jnp.where(col < limit, s, NEG)
        peak = jnp.maximum(jnp.max(s, axis=1, keepdims=True), FLOOR)
        p = jnp.exp2(s - peak)
        total = jnp.sum(p, axis=1, keepdims=True)
        mixed = jnp.dot(
            p.astype(jnp.bfloat16), tvb[r, :, low : low + HSIZE], preferred_element_type=jnp.float32
        )
        return peak, total, mixed

    part_copies = {}

    def cross(r):
        for copy in text_copies[r]:
            copy.wait()
        if r == 0:
            own_cq.wait()
        else:
            cq_copies[r].wait_recv()
        stats = []
        for h in range(H):
            low = h * HSIZE
            peak, total, mixed = cross_head(r, h)
            if r == 0:
                cown[:, low : low + HSIZE] = mixed
                ctop[h] = peak
                ctot[h] = total
            else:
                part_out[r, :, low : low + HSIZE] = mixed.astype(jnp.bfloat16)
                stats += [peak, total]
        if r > 0:
            cstat_out[r] = pack_stats(stats)
            pair = (
                remote(part_out.at[r], part_in.at[r], part_send.at[r, 0], part_recv.at[r, 0], (me, owners[r])),
                remote(cstat_out.at[r], cstat_in.at[r], part_send.at[r, 1], part_recv.at[r, 1], (me, owners[r])),
            )
            for copy in pair:
                copy.start()
            part_copies[r] = pair

    def first_half(h, half):
        part = pl.ds(half * rows, rows)
        s = scores_of(qp[h, part], kbuf[0, h])
        if half == 0:
            i = lax.broadcasted_iota(jnp.int32, (rows, rows), 0)
            j = lax.broadcasted_iota(jnp.int32, (rows, rows), 1)
            s = jnp.where(j <= i, s, NEG)
        else:
            s = s + y.astype(jnp.float32) * NEG
        peak = jnp.maximum(jnp.max(s, axis=1, keepdims=True), FLOOR)
        p = jnp.exp2(s - peak)
        top[h, part] = peak
        tot[h, part] = jnp.sum(p, axis=1, keepdims=True)
        acc[h, part] = jnp.dot(
            p.astype(jnp.bfloat16), vbuf[0, h], preferred_element_type=jnp.float32
        )

    def item(n, carry):
        d = n // H + 1
        h = n % H
        kv_copy(d - 1, h, 0).wait_recv()
        kv_copy(d - 1, h, 1).wait_recv()

        @pl.when(z < nz - 1)
        def _():
            kv_copy(d, h, 0).start()
            kv_copy(d, h, 1).start()

        for half in range(2):
            part = pl.ds(half * rows, rows)
            s = scores_of(qp[h, part], kbuf[d, h])
            before = top[h, part]
            peak = jnp.maximum(before, jnp.max(s, axis=1, keepdims=True))
            p = jnp.exp2(s - peak)
            shrink = jnp.exp2(before - peak)
            top[h, part] = peak
            tot[h, part] = tot[h, part] * shrink + jnp.sum(p, axis=1, keepdims=True)
            acc[h, part] = acc[h, part] * shrink + jnp.dot(
                p.astype(jnp.bfloat16), vbuf[d, h], preferred_element_type=jnp.float32
            )
        return carry

    items = H * z
    cross(0)
    if T > 1:
        cross(1)
    for copy in locals_:
        copy.wait()
    for h in range(H):
        first_half(h, 0)
    for copy in q_copies:
        copy.wait_recv()
    for h in range(H):
        first_half(h, 1)
    done = 0
    for r in range(2, T):
        lax.fori_loop(jnp.minimum(done, items), jnp.minimum(done + 2, items), item, 0)
        done += 2
        cross(r)
    lax.fori_loop(jnp.minimum(done, items), items, item, 0)

    theirs = pl.ds(rows, rows)
    mine = pl.ds(0, rows)
    pair_copies = []
    for h in range(H):
        pair_out[h] = acc[h, theirs].astype(jnp.bfloat16)
        pstat_out[h] = pack_stats([top[h, theirs], tot[h, theirs]])
        for copy in (
            remote(pair_out.at[h], pair_in.at[h], pair_send.at[h, 0], pair_recv.at[h, 0], (partner, t)),
            remote(pstat_out.at[h], pstat_in.at[h], pair_send.at[h, 1], pair_recv.at[h, 1], (partner, t)),
        ):
            copy.start()
            pair_copies.append(copy)

    arrived = []
    for r in range(1, T):
        for copy in part_copies[r]:
            copy.wait_recv()
        arrived.append(unpack_stats(cstat_in[r], 2 * H))
    for h in range(H):
        low = h * HSIZE
        peak = ctop[h]
        for stats in arrived:
            peak = jnp.maximum(peak, stats[2 * h])
        weight = jnp.exp2(ctop[h] - peak)
        total = ctot[h] * weight
        mixed = cown[:, low : low + HSIZE] * weight
        for r in range(1, T):
            weight = jnp.exp2(arrived[r - 1][2 * h] - peak)
            total = total + arrived[r - 1][2 * h + 1] * weight
            mixed = mixed + part_in[r, :, low : low + HSIZE].astype(jnp.float32) * weight
        cross_out[:, low : low + HSIZE] = (mixed / total).astype(jnp.bfloat16)

    for h in range(H):
        low = h * HSIZE
        pair_copies[2 * h].wait_recv()
        pair_copies[2 * h + 1].wait_recv()
        other_top, other_tot = unpack_stats(pstat_in[h], 2)
        peak = jnp.maximum(top[h, mine], other_top)
        a = jnp.exp2(top[h, mine] - peak)
        b = jnp.exp2(other_top - peak)
        total = tot[h, mine] * a + other_tot * b
        mixed = acc[h, mine] * a + pair_in[h].astype(jnp.float32) * b
        self_out[:, low : low + HSIZE] = (mixed / total).astype(jnp.bfloat16)

    for copy in pair_copies + q_copies + cq_copies[1:]:
        copy.wait_send()
    for r in range(1, T):
        for copy in part_copies[r]:
            copy.wait_send()

    @pl.when(z < nz - 1)
    def _():
        for h in range(H):
            own_kv(h, 0).wait_send()
            own_kv(h, 1).wait_send()

        def drain(n, carry):
            kv_copy(n // H + 1, n % H, 0).wait_send()
            kv_copy(n // H + 1, n % H, 1).wait_send()
            return carry

        lax.fori_loop(0, items, drain, 0)


def per_device(S, T, self_q, self_k, self_v, cross_q, text_k, text_v, lags):
    rows, width = self_q.shape
    text = text_k.shape[0]
    H = width // HSIZE
    nz = S // 2
    bf16, f32 = jnp.bfloat16, jnp.float32
    vmem = pltpu.VMEM
    dma = pltpu.SemaphoreType.DMA
    any_spec = pl.BlockSpec(memory_space=pl.ANY)
    return pl.pallas_call(
        functools.partial(kernel, S, T, rows, H, text),
        out_shape=(jax.ShapeDtypeStruct((rows, width), bf16),) * 2,
        in_specs=[pl.BlockSpec(memory_space=pltpu.SMEM)] + [any_spec] * 6,
        out_specs=(pl.BlockSpec(memory_space=vmem),) * 2,
        scratch_shapes=[
            vmem((H, 2 * rows, HSIZE), bf16),
            vmem((nz, H, rows, HSIZE), bf16),
            vmem((nz, H, rows, HSIZE), bf16),
            vmem((H, 2 * rows, HSIZE), f32),
            vmem((H, 2 * rows, 1), f32),
            vmem((H, 2 * rows, 1), f32),
            vmem((H, rows, HSIZE), bf16),
            vmem((H, rows, HSIZE), bf16),
            vmem((H, 8, rows), f32),
            vmem((H, 8, rows), f32),
            vmem((T, rows, width), bf16),
            vmem((T, text, width), bf16),
            vmem((T, text, width), bf16),
            vmem((rows, width), f32),
            vmem((H, rows, 1), f32),
            vmem((H, rows, 1), f32),
            vmem((T, rows, width), bf16),
            vmem((T, rows, width), bf16),
            vmem((T, 8, rows), f32),
            vmem((T, 8, rows), f32),
            dma((1 + 3 * H,)),
            dma((T, 2)),
            dma((H,)),
            dma((H,)),
            dma((nz, H, 2)),
            dma((nz + 1, H, 2)),
            dma((T,)),
            dma((T,)),
            dma((H, 2)),
            dma((H, 2)),
            dma((T, 2)),
            dma((T, 2)),
        ],
        compiler_params=pltpu.CompilerParams(
            collective_id=0, has_side_effects=True, vmem_limit_bytes=48 * 1024 * 1024
        ),
        cost_estimate=pl.CostEstimate(
            flops=4 * rows * width * (T * text + nz * 2 * rows),
            bytes_accessed=4 * text * T * width,
            transcendentals=rows * H * (T * text + nz * 2 * rows),
        ),
    )(lags, self_q, self_k, self_v, cross_q, text_k, text_v)


def solution(mesh):
    S, T = mesh.shape["seq"], mesh.shape["txt"]
    return jax.shard_map(
        functools.partial(per_device, S, T),
        mesh=mesh,
        in_specs=(
            P("seq", "txt"),
            P("seq", "txt"),
            P("seq", "txt"),
            P("seq", "txt"),
            P("txt", None),
            P("txt", None),
            P("seq"),
        ),
        out_specs=(P("seq", "txt"), P("seq", "txt")),
        check_vma=False,
    )
```
